32 devices in a mesh: scen: 4 (over y, x), intr: 8 (over z, core).
Axes of the slice: x: 2, y: 2, z: 4, core: 2. Of those that a mesh axis runs over, the one named last changes fastest.
Arguments:
- inverse_panels: bfloat16 [16, 2048, 2048], P('scen', 'intr'), may hold values from -0.125 to 0.125
- border_columns: bfloat16 [16, 2048, 512], P('scen', 'intr'), may hold values from -6 to 6
- border_tiles: bfloat16 [16, 16, 2048, 128], P('scen', None, 'intr'), may hold values from -0.125 to 0.125
- tile_rows: int32 [16, 16], P('scen'), may hold values from 0 to 31
- tile_slabs: int32 [16, 16], P('scen'), may hold values from 0 to 1
- tile_count: int32 [16], P('scen'), may hold values from 1 to 16
- base_slab: float32 [4096, 512], P(('scen', 'intr')), may hold values from -6 to 6
- earlier_panels: bfloat16 [8, 4096, 128], P(None, ('scen', 'intr')), may hold values from -0.25 to 0.25
- used_panels: int32 [4], replicated, may hold values from 0 to 7, as said below
Outputs:
- schur_slab: float32 [4096, 512], P(('scen', 'intr'))
The draws below stay inside these ranges and needn't reach their ends.
Inputs may be any that keep to these rules, and one draw needn't show every extreme that they name: `used_panels`: distinct panel ids.
All inputs are finite; a program needn't handle non-finite values.
Results may differ from the reference program's by a relative error of at most 0.0026.
Values may be sent and summed in bfloat16 or wider, within the bound.
A program may use at most 128 MiB of HBM per device.

```python
import jax
import jax.numpy as jnp
from jax import lax

SLAB_ROWS = 4096
COLS = 512
SLAB_W = 256
TILE = 128
LIST = 16
PANELS = 8
USED = 4
ROWS = 2048
SCEN = 16
NTILE = 32
NSLAB = 2


def draw_used_panels(key, part):
    return jax.random.permutation(key, PANELS)[:USED].astype(jnp.int32)


def with_ends(drawn, own_key, smallest, top_value):
    longest = drawn.shape.index(max(drawn.shape))
    spots = []
    for shift in (0, 1):
        where = [jax.random.randint(jax.random.fold_in(own_key, axis), (), 0, length) for axis, length in enumerate(drawn.shape)]
        where[longest] = (where[longest] + shift) % drawn.shape[longest]
        spots.append(tuple(where))
    return drawn.at[spots[0]].set(smallest).at[spots[1]].set(top_value)


def block_levels(own_key, shape, pieces, low, top_value):
    def one(axis_at, shards_of):
        draws = jax.random.uniform(jax.random.fold_in(jax.random.fold_in(own_key, 6), axis_at), (shards_of,), jnp.float32, low / len(pieces), top_value / len(pieces))
        return jnp.repeat(jnp.exp(draws), shape[axis_at] // shards_of).reshape((-1,) + (1,) * (len(shape) - axis_at - 1))

    gain = one(*pieces[0])
    for cut in pieces[1:]:
        gain = gain * one(*cut)
    return gain


def gaussian(own_key, shape, width, reach, shards=(), kind=jnp.bfloat16):
    drawn = jax.random.normal(own_key, shape, jnp.float32) * width
    if len(shards) > 0:
        drawn = block_levels(own_key, shape, shards, -0.22, 0.18) * drawn
    return jnp.clip(drawn, min=-reach, max=reach).astype(kind)


def setup_inputs(seed: int = 0) -> dict:
    key_list = jax.random.split(jax.random.key(seed), 10)
    inverse_panels = gaussian(key_list[0], (SCEN, ROWS, ROWS), ROWS ** -0.5, 0.125, ((0, 4), (1, 8)))
    border_columns = gaussian(key_list[1], (SCEN, ROWS, COLS), 1.0, 6.0, ((0, 4), (1, 8)))
    border_tiles = gaussian(key_list[2], (SCEN, LIST, ROWS, TILE), ROWS ** -0.5, 0.125, ((0, 4), (2, 8)))
    tile_rows = with_ends(jax.random.randint(key_list[3], (SCEN, LIST), 0, NTILE), jax.random.fold_in(key_list[3], 1), 0, NTILE - 1).astype(jnp.int32)
    tile_slabs = with_ends(jax.random.randint(key_list[4], (SCEN, LIST), 0, NSLAB), jax.random.fold_in(key_list[4], 1), 0, NSLAB - 1).astype(jnp.int32)
    tile_count = with_ends(jax.random.randint(key_list[5], (SCEN,), 1, LIST + 1), jax.random.fold_in(key_list[5], 1), 1, LIST).astype(jnp.int32)
    base_slab = gaussian(key_list[6], (SLAB_ROWS, COLS), 1.0, 6.0, ((0, 32),), jnp.float32)
    earlier_panels = gaussian(key_list[7], (PANELS, SLAB_ROWS, TILE), (USED * TILE) ** -0.5, 0.25, ((1, 32),))
    used_panels = draw_used_panels(jax.random.fold_in(key_list[9], 71), 0)
    return dict(inverse_panels=inverse_panels, border_columns=border_columns, border_tiles=border_tiles, tile_rows=tile_rows, tile_slabs=tile_slabs, tile_count=tile_count, base_slab=base_slab, earlier_panels=earlier_panels, used_panels=used_panels)


def reference(inverse_panels, border_columns, border_tiles, tile_rows, tile_slabs, tile_count, base_slab, earlier_panels, used_panels):
    nslab = COLS // SLAB_W
    targets = jnp.arange(NTILE * nslab, dtype=jnp.int32)
    positions = jnp.arange(LIST, dtype=jnp.int32)

    def one_scenario(total, items):
        inverse, columns, tiles, rows, slabs, count = items
        applied = jnp.dot(inverse, columns, preferred_element_type=jnp.float32).astype(jnp.bfloat16)
        split = applied.reshape(ROWS, nslab, SLAB_W)
        chosen = jnp.transpose(split[:, slabs, :], (1, 0, 2))
        product = jnp.einsum('lrt,lrw->ltw', tiles.astype(jnp.float32), chosen.astype(jnp.float32))
        live = (positions < count).astype(jnp.float32)
        places = (rows * nslab + slabs).astype(jnp.int32)
        onehot = (places[:, None] == targets[None, :]).astype(jnp.float32) * live[:, None]
        block = jnp.dot(onehot.T, product.reshape(LIST, TILE * SLAB_W), precision=lax.Precision.HIGHEST)
        return total + block, None

    start = jnp.zeros((NTILE * nslab, TILE * SLAB_W), jnp.float32)
    total, unused = lax.scan(one_scenario, start, (inverse_panels, border_columns, border_tiles, tile_rows, tile_slabs, tile_count))
    coupling = total.reshape(NTILE, nslab, TILE, SLAB_W).transpose(0, 2, 1, 3).reshape(SLAB_ROWS, COLS)
    chosen_panels = earlier_panels[used_panels].astype(jnp.float32)
    earlier = jnp.einsum('prt,pct->rc', chosen_panels, chosen_panels[:, :COLS, :])
    return base_slab - coupling - earlier
```

```python
import functools

import jax
import jax.numpy as jnp
from jax import lax
from jax.experimental import pallas as pl
from jax.experimental.pallas import tpu as pltpu
from jax.sharding import PartitionSpec as P

SLAB_W = 256
TILE = 128
WIDTH = 128
MESH = pl.DeviceIdType.MESH
F32 = jnp.float32
BF16 = jnp.bfloat16


def kernel(
    groups,
    inner,
    used_ref,
    prev_ref,
    last_ref,
    inv_hbm,
    cols_hbm,
    tiles_hbm,
    base_hbm,
    panels_hbm,
    out_hbm,
    inv,
    gath,
    tiles,
    turned,
    base,
    panels,
    own_top,
    top,
    earlier,
    applied,
    chain,
    keep,
    pair_out,
    pair_in,
    mid,
    scen_out,
    scen_in,
    low,
    line_out,
    line_in,
    result,
    load_sem,
    own_sem,
    col_send,
    col_recv,
    hop_send,
    hop_recv,
    top_send,
    top_recv,
    pair_send,
    pair_recv,
    scen_send,
    scen_recv,
    line_send,
    line_recv,
    out_sem,
):
    scen_here, listed, rows, _ = tiles.shape
    mine_rows, cols = base.shape
    used = own_top.shape[0]
    chunks = cols // WIDTH
    zs = inner // 2
    sub = TILE // mine_rows
    nslab = cols // SLAB_W
    tops = cols // mine_rows
    me_s = lax.axis_index("scen")
    me_i = lax.axis_index("intr")
    z, c = me_i // 2, me_i % 2
    sibling = (me_s, z * 2 + 1 - c)

    def remote(src, dst, send, recv, device):
        return pltpu.make_async_remote_copy(
            src_ref=src, dst_ref=dst, send_sem=send, recv_sem=recv, device_id=device, device_id_type=MESH
        )

    loads = [
        pltpu.make_async_copy(src, dst, load_sem.at[n])
        for n, (src, dst) in enumerate(
            [(panels_hbm, panels), (tiles_hbm, tiles), (inv_hbm, inv), (base_hbm, base)]
        )
    ]
    for load in loads:
        load.start()

    barrier = pltpu.get_barrier_semaphore()
    partners = [(lax.rem(me_s + n, groups), me_i) for n in range(1, groups)]
    partners += [(me_s, lax.rem(z + n, zs) * 2 + c) for n in range(1, zs)]
    partners += [sibling]
    for partner in partners:
        pl.semaphore_signal(barrier, inc=1, device_id=partner, device_id_type=MESH)
    pl.semaphore_wait(barrier, len(partners))

    def slot(q, j):
        return gath.at[q, :, pl.ds(pl.multiple_of(j * rows, rows), rows), :]

    def own_block(q):
        return cols_hbm.at[:, :, pl.ds(q * WIDTH, WIDTH)]

    def col_copy(q, j, way, src):
        device = [(me_s, (z + 1) * 2 + c), (me_s, (z - 1) * 2 + c), sibling][way]
        return remote(src, slot(q, j), col_send.at[q, j, way], col_recv.at[q, j], device)

    def own_local(q):
        return pltpu.make_async_copy(own_block(q), slot(q, me_i), own_sem.at[q])

    def own_start(q):
        @pl.when(z < zs - 1)
        def _():
            col_copy(q, me_i, 0, own_block(q)).start()

        @pl.when(z > 0)
        def _():
            col_copy(q, me_i, 1, own_block(q)).start()

        col_copy(q, me_i, 2, own_block(q)).start()
        own_local(q).start()

    def top_slot(j):
        return top.at[:, pl.ds(pl.multiple_of(j * mine_rows, mine_rows), mine_rows), :]

    def top_copy(j, way):
        device = [(me_s, (z + 1) * 2 + c), (me_s, (z - 1) * 2 + c), sibling][way]
        return remote(top_slot(j), top_slot(j), top_send.at[j, way], top_recv.at[j], device)

    def pass_on(copy, d, has):
        @pl.when((z >= d) & has(z - d))
        def _():
            j = (z - d) * 2 + c
            copy(j, 0).wait_recv()

            @pl.when(z < zs - 1)
            def _():
                copy(j, 0).start()

            copy(j, 2).start()

        @pl.when((z + d < zs) & has(z + d))
        def _():
            j = (z + d) * 2 + c
            copy(j, 1).wait_recv()

            @pl.when(z > 0)
            def _():
                copy(j, 1).start()

            copy(j, 2).start()

    def relay(q, d):
        pass_on(lambda j, way: col_copy(q, j, way, slot(q, j)), d, lambda other: other >= 0)

    def has_top(other):
        return other < tops // 2

    def hop(n):
        return remote(
            own_top, top_slot(me_i), hop_send.at[n], hop_recv, (lax.rem(me_s + n, groups), me_i)
        )

    def top_local():
        return pltpu.make_async_copy(own_top, top_slot(me_i), load_sem.at[len(loads)])

    def pair_copy(q):
        return remote(pair_out.at[q], pair_in.at[q], pair_send.at[q], pair_recv.at[q], sibling)

    def scen_copy(q, n):
        return remote(
            scen_out.at[q, n - 1],
            scen_in.at[q, n - 1],
            scen_send.at[q, n - 1],
            scen_recv.at[q, n - 1],
            (lax.rem(me_s + n, groups), me_i),
        )

    def line_copy(q, n):
        return remote(
            line_out.at[q, n - 1],
            line_in.at[q, n - 1],
            line_send.at[q, n - 1],
            line_recv.at[q, n - 1],
            (me_s, lax.rem(z + n, zs) * 2 + c),
        )

    def compute(q):
        def apply(s, carry):
            applied[s] = jnp.dot(inv[s], gath[q, s], preferred_element_type=F32).astype(BF16)
            return carry

        lax.fori_loop(0, scen_here, apply, 0)
        batch = 4

        def multiply(s, carry):
            for n in range(listed // batch):
                product = jnp.dot(
                    turned[s, n * batch * TILE : (n + 1) * batch * TILE, :],
                    applied[s],
                    preferred_element_type=F32,
                )
                for m in range(batch):
                    e = s * listed + n * batch + m
                    block = product[m * TILE : (m + 1) * TILE].reshape(sub, mine_rows, WIDTH)
                    chain[e + 1] = block + chain[prev_ref[e]]
            return carry

        lax.fori_loop(0, scen_here, multiply, 0)
        slab = q * WIDTH // SLAB_W

        def place(k, carry):
            mine, other = 2 * k + c, 2 * k + 1 - c
            pair_out[q, k] = chain[last_ref[other // sub * nslab + slab], other % sub]
            keep[k] = chain[last_ref[mine // sub * nslab + slab], mine % sub]
            return carry

        lax.fori_loop(0, groups * zs, place, 0)
        pair_copy(q).start()

    def to_groups(q):
        pair_copy(q).wait_recv()
        for n in list(range(1, groups)) + [0]:
            at = pl.ds(lax.rem(me_s + n, groups) * zs, zs)
            block = keep[at] + pair_in[q, at]
            if n == 0:
                mid[q] = block
            else:
                scen_out[q, n - 1] = block.astype(BF16)
                scen_copy(q, n).start()

    def to_line(q):
        for n in range(1, groups):
            scen_copy(q, n).wait_recv()
        total = mid[q]
        for n in range(1, groups):
            total += scen_in[q, n - 1].astype(F32)
        low[q] = total
        for n in range(1, zs):
            line_out[q, n - 1] = low[q, lax.rem(z + n, zs)].astype(BF16)
            line_copy(q, n).start()

    def out_copy(q):
        at = pl.ds(q * WIDTH, WIDTH)
        return pltpu.make_async_copy(result.at[q], out_hbm.at[:, at], out_sem.at[q])

    def finish(q):
        at = slice(q * WIDTH, (q + 1) * WIDTH)
        total = low[q, z]
        for n in range(1, zs):
            line_copy(q, n).wait_recv()
            total += line_in[q, n - 1].astype(F32)
        result[q] = base[:, at] - total - earlier[:, at]
        out_copy(q).start()

    own_start(0)
    loads[0].wait()
    for p in range(used):
        own_top[p] = panels[used_ref[p]]

    @pl.when((me_s == 0) & (me_i < tops))
    def _():
        for n in range(1, groups):
            hop(n).start()
        top_local().start()

    loads[1].wait()

    def turn(s, carry):
        for n in range(listed):
            turned[s, n * TILE : (n + 1) * TILE, :] = tiles[s, n].T
        return carry

    lax.fori_loop(0, scen_here, turn, 0)
    chain[0] = jnp.zeros(chain.shape[1:], F32)
    loads[2].wait()
    loads[3].wait()

    for q in range(chunks):
        if q + 1 < chunks:
            own_start(q + 1)
        for d in range(1, zs):
            relay(q, d)
            if q > 0 and d == 1:
                to_line(q - 1)
        if q == 0:

            @pl.when(me_i < tops)
            def _():
                @pl.when(me_s == 0)
                def _():
                    top_local().wait()

                @pl.when(me_s > 0)
                def _():
                    hop(1).wait_recv()

                @pl.when(z < zs - 1)
                def _():
                    top_copy(me_i, 0).start()

                @pl.when(z > 0)
                def _():
                    top_copy(me_i, 1).start()

                top_copy(me_i, 2).start()

            for d in range(1, zs):
                pass_on(top_copy, d, has_top)
        else:
            finish(q - 1)
        own_local(q).wait()
        for other in range(zs):
            col_copy(q, other * 2 + 1 - c, 2, slot(q, other * 2 + 1 - c)).wait_recv()
        compute(q)
        if q == 0:
            for other in range(tops // 2):
                top_copy(other * 2 + 1 - c, 2).wait_recv()
            total = jnp.zeros((mine_rows, cols), F32)
            for p in range(used):
                total += lax.dot_general(
                    own_top[p], top[p], (((1,), (1,)), ((), ())), preferred_element_type=F32
                )
            earlier[...] = total
        to_groups(q)
    to_line(chunks - 1)
    finish(chunks - 1)

    def drain(copy, other):
        j = other * 2 + c

        @pl.when((z >= other) & (z < zs - 1))
        def _():
            copy(j, 0).wait_send()

        @pl.when((z <= other) & (z > 0))
        def _():
            copy(j, 1).wait_send()

        copy(j, 2).wait_send()

    def drain_chunk(q, carry):
        def one(other, inside):
            drain(lambda j, way: col_copy(q, j, way, slot(q, j)), other)
            return inside

        lax.fori_loop(0, zs, one, 0)
        pair_copy(q).wait_send()
        for n in range(1, groups):
            scen_copy(q, n).wait_send()
        for n in range(1, zs):
            line_copy(q, n).wait_send()
        return carry

    lax.fori_loop(0, chunks, drain_chunk, 0)
    for other in range(tops // 2):
        drain(top_copy, other)

    @pl.when((me_s == 0) & (me_i < tops))
    def _():
        for n in range(1, groups):
            hop(n).wait_send()

    for q in range(chunks):
        out_copy(q).wait()


def on_device(
    groups,
    inner,
    inverse_panels,
    border_columns,
    border_tiles,
    tile_rows,
    tile_slabs,
    tile_count,
    base_slab,
    earlier_panels,
    used_panels,
):
    scen_here, rows, depth = inverse_panels.shape
    cols = border_columns.shape[2]
    listed = border_tiles.shape[1]
    mine_rows = base_slab.shape[0]
    used = used_panels.shape[0]
    nslab = cols // SLAB_W
    chunks = cols // WIDTH
    zs = inner // 2
    sub = TILE // mine_rows
    tops = cols // mine_rows
    entries = scen_here * listed
    targets = mine_rows * groups * inner // TILE * nslab
    live = jnp.arange(listed, dtype=jnp.int32)[None, :] < tile_count[:, None]
    keys = jnp.where(live, tile_rows * nslab + tile_slabs, -1).reshape(entries)
    at = jnp.arange(entries, dtype=jnp.int32)
    same = (keys[None, :] == keys[:, None]) & (at[None, :] < at[:, None])
    prev = jnp.max(jnp.where(same, at[None, :] + 1, 0), axis=1)
    hits = keys[None, :] == jnp.arange(targets, dtype=jnp.int32)[:, None]
    last = jnp.max(jnp.where(hits, at[None, :] + 1, 0), axis=1)
    dma = pltpu.SemaphoreType.DMA
    smem = pl.BlockSpec(memory_space=pltpu.SMEM)
    anywhere = pl.BlockSpec(memory_space=pl.ANY)
    return pl.pallas_call(
        functools.partial(kernel, groups, inner),
        out_shape=jax.ShapeDtypeStruct((mine_rows, cols), F32),
        in_specs=[smem] * 3 + [anywhere] * 5,
        out_specs=anywhere,
        scratch_shapes=[
            pltpu.VMEM((scen_here, rows, depth), BF16),
            pltpu.VMEM((chunks, scen_here, depth, WIDTH), BF16),
            pltpu.VMEM(border_tiles.shape, BF16),
            pltpu.VMEM((scen_here, listed * TILE, rows), BF16),
            pltpu.VMEM((mine_rows, cols), F32),
            pltpu.VMEM(earlier_panels.shape, BF16),
            pltpu.VMEM((used, mine_rows, TILE), BF16),
            pltpu.VMEM((used, cols, TILE), BF16),
            pltpu.VMEM((mine_rows, cols), F32),
            pltpu.VMEM((scen_here, rows, WIDTH), BF16),
            pltpu.VMEM((entries + 1, sub, mine_rows, WIDTH), F32),
            pltpu.VMEM((groups * zs, mine_rows, WIDTH), F32),
            pltpu.VMEM((chunks, groups * zs, mine_rows, WIDTH), F32),
            pltpu.VMEM((chunks, groups * zs, mine_rows, WIDTH), F32),
            pltpu.VMEM((chunks, zs, mine_rows, WIDTH), F32),
            pltpu.VMEM((chunks, groups - 1, zs, mine_rows, WIDTH), BF16),
            pltpu.VMEM((chunks, groups - 1, zs, mine_rows, WIDTH), BF16),
            pltpu.VMEM((chunks, zs, mine_rows, WIDTH), F32),
            pltpu.VMEM((chunks, zs - 1, mine_rows, WIDTH), BF16),
            pltpu.VMEM((chunks, zs - 1, mine_rows, WIDTH), BF16),
            pltpu.VMEM((chunks, mine_rows, WIDTH), F32),
            dma((5,)),
            dma((chunks,)),
            dma((chunks, inner, 3)),
            dma((chunks, inner)),
            dma((groups,)),
            dma,
            dma((tops, 3)),
            dma((tops,)),
            dma((chunks,)),
            dma((chunks,)),
            dma((chunks, groups - 1)),
            dma((chunks, groups - 1)),
            dma((chunks, zs - 1)),
            dma((chunks, zs - 1)),
            dma((chunks,)),
        ],
        compiler_params=pltpu.CompilerParams(
            collective_id=0, has_side_effects=True, vmem_limit_bytes=60 * 1024 * 1024
        ),
        cost_estimate=pl.CostEstimate(
            flops=2 * scen_here * rows * cols * (depth + listed * TILE // nslab),
            bytes_accessed=2 * scen_here * rows * (depth + listed * TILE + cols),
            transcendentals=0,
        ),
    )(
        used_panels,
        prev,
        last,
        inverse_panels,
        border_columns,
        border_tiles,
        base_slab,
        earlier_panels,
    )


def solution(mesh):
    groups, inner = mesh.shape["scen"], mesh.shape["intr"]
    return jax.shard_map(
        functools.partial(on_device, groups, inner),
        mesh=mesh,
        in_specs=(
            P("scen", "intr", None),
            P("scen", "intr", None),
            P("scen", None, "intr", None),
            P("scen", None),
            P("scen", None),
            P("scen"),
            P(("scen", "intr"), None),
            P(None, ("scen", "intr"), None),
            P(),
        ),
        out_specs=P(("scen", "intr"), None),
        check_vma=False,
    )
```

```python
import functools

import jax
import jax.numpy as jnp
from jax import lax
from jax.experimental import pallas as pl
from jax.experimental.pallas import tpu as pltpu
from jax.sharding import PartitionSpec as P

SLAB_W = 256
TILE = 128
WIDTH = 128
MESH = pl.DeviceIdType.MESH
F32 = jnp.float32
BF16 = jnp.bfloat16


def kernel(
    groups,
    inner,
    used_ref,
    prev_ref,
    last_ref,
    inv_hbm,
    cols_hbm,
    tiles_hbm,
    base_hbm,
    panels_hbm,
    out_hbm,
    inv,
    gath,
    tiles,
    turned,
    base,
    panels,
    own_top,
    top,
    earlier,
    applied,
    chain,
    keep,
    pair_out,
    pair_in,
    mid,
    scen_out,
    scen_in,
    low,
    line_out,
    line_in,
    result,
    load_sem,
    own_sem,
    col_send,
    col_recv,
    hop_send,
    hop_recv,
    top_send,
    top_recv,
    pair_send,
    pair_recv,
    scen_send,
    scen_recv,
    line_send,
    line_recv,
    out_sem,
):
    scen_here, listed, rows, _ = tiles.shape
    mine_rows, cols = base.shape
    used = own_top.shape[0]
    chunks = cols // WIDTH
    zs = inner // 2
    sub = TILE // mine_rows
    nslab = cols // SLAB_W
    tops = cols // mine_rows
    me_s = lax.axis_index("scen")
    me_i = lax.axis_index("intr")
    z, c = me_i // 2, me_i % 2
    sibling = (me_s, z * 2 + 1 - c)

    def remote(src, dst, send, recv, device):
        return pltpu.make_async_remote_copy(
            src_ref=src, dst_ref=dst, send_sem=send, recv_sem=recv, device_id=device, device_id_type=MESH
        )

    loads = [
        pltpu.make_async_copy(src, dst, load_sem.at[n])
        for n, (src, dst) in enumerate(
            [(panels_hbm, panels), (tiles_hbm, tiles), (inv_hbm, inv), (base_hbm, base)]
        )
    ]
    for load in loads:
        load.start()

    barrier = pltpu.get_barrier_semaphore()
    partners = [(lax.rem(me_s + n, groups), me_i) for n in range(1, groups)]
    partners += [(me_s, lax.rem(z + n, zs) * 2 + c) for n in range(1, zs)]
    partners += [sibling]
    for partner in partners:
        pl.semaphore_signal(barrier, inc=1, device_id=partner, device_id_type=MESH)
    pl.semaphore_wait(barrier, len(partners))

    def slot(q, j):
        return gath.at[q, :, pl.ds(pl.multiple_of(j * rows, rows), rows), :]

    def own_block(q):
        return cols_hbm.at[:, :, pl.ds(q * WIDTH, WIDTH)]

    def col_copy(q, j, way, src):
        device = [(me_s, (z + 1) * 2 + c), (me_s, (z - 1) * 2 + c), sibling][way]
        return remote(src, slot(q, j), col_send.at[q, j, way], col_recv.at[q, j], device)

    def own_local(q):
        return pltpu.make_async_copy(own_block(q), slot(q, me_i), own_sem.at[q])

    def own_start(q):
        @pl.when(z < zs - 1)
        def _():
            col_copy(q, me_i, 0, own_block(q)).start()

        @pl.when(z > 0)
        def _():
            col_copy(q, me_i, 1, own_block(q)).start()

        col_copy(q, me_i, 2, own_block(q)).start()
        own_local(q).start()

    def top_slot(j):
        return top.at[:, pl.ds(pl.multiple_of(j * mine_rows, mine_rows), mine_rows), :]

    def top_copy(j, way):
        device = [(me_s, (z + 1) * 2 + c), (me_s, (z - 1) * 2 + c), sibling][way]
        return remote(top_slot(j), top_slot(j), top_send.at[j, way], top_recv.at[j], device)

    def pass_on(copy, d, has):
        @pl.when((z >= d) & has(z - d))
        def _():
            j = (z - d) * 2 + c
            copy(j, 0).wait_recv()

            @pl.when(z < zs - 1)
            def _():
                copy(j, 0).start()

            copy(j, 2).start()

        @pl.when((z + d < zs) & has(z + d))
        def _():
            j = (z + d) * 2 + c
            copy(j, 1).wait_recv()

            @pl.when(z > 0)
            def _():
                copy(j, 1).start()

            copy(j, 2).start()

    def relay(q, d):
        pass_on(lambda j, way: col_copy(q, j, way, slot(q, j)), d, lambda other: other >= 0)

    def has_top(other):
        return other < tops // 2

    def hop(n):
        return remote(
            own_top, top_slot(me_i), hop_send.at[n], hop_recv, (lax.rem(me_s + n, groups), me_i)
        )

    def top_local():
        return pltpu.make_async_copy(own_top, top_slot(me_i), load_sem.at[len(loads)])

    def pair_copy(q, n):
        at = pl.ds(lax.rem(me_s + n, groups) * zs, zs)
        return remote(
            pair_out.at[q, at], pair_in.at[q, at], pair_send.at[q, n], pair_recv.at[q, n], sibling
        )

    def scen_copy(q, n):
        return remote(
            scen_out.at[q, n - 1],
            scen_in.at[q, n - 1],
            scen_send.at[q, n - 1],
            scen_recv.at[q, n - 1],
            (lax.rem(me_s + n, groups), me_i),
        )

    def line_copy(q, n):
        return remote(
            line_out.at[q, n - 1],
            line_in.at[q, n - 1],
            line_send.at[q, n - 1],
            line_recv.at[q, n - 1],
            (me_s, lax.rem(z + n, zs) * 2 + c),
        )

    def compute(q):
        def apply(s, carry):
            applied[s] = jnp.dot(inv[s], gath[q, s], preferred_element_type=F32).astype(BF16)
            return carry

        lax.fori_loop(0, scen_here, apply, 0)
        batch = 4

        def multiply(s, carry):
            for n in range(listed // batch):
                product = jnp.dot(
                    turned[s, n * batch * TILE : (n + 1) * batch * TILE, :],
                    applied[s],
                    preferred_element_type=F32,
                )
                for m in range(batch):
                    e = s * listed + n * batch + m
                    block = product[m * TILE : (m + 1) * TILE].reshape(sub, mine_rows, WIDTH)
                    chain[e + 1] = block + chain[prev_ref[e]]
            return carry

        lax.fori_loop(0, scen_here, multiply, 0)
        slab = q * WIDTH // SLAB_W

        def place(k, carry):
            mine, other = 2 * k + c, 2 * k + 1 - c
            pair_out[q, k] = chain[last_ref[other // sub * nslab + slab], other % sub]
            keep[k] = chain[last_ref[mine // sub * nslab + slab], mine % sub]
            return carry

        for n in list(range(1, groups)) + [0]:
            first = lax.rem(me_s + n, groups) * zs
            lax.fori_loop(first, first + zs, place, 0)
            pair_copy(q, n).start()

    def to_groups(q):
        for n in list(range(1, groups)) + [0]:
            at = pl.ds(lax.rem(me_s + n, groups) * zs, zs)
            pair_copy(q, n).wait_recv()
            block = keep[at] + pair_in[q, at]
            if n == 0:
                mid[q] = block
            else:
                scen_out[q, n - 1] = block.astype(BF16)
                scen_copy(q, n).start()

    def to_line(q):
        for n in range(1, groups):
            scen_copy(q, n).wait_recv()
        total = mid[q]
        for n in range(1, groups):
            total += scen_in[q, n - 1].astype(F32)
        low[q] = total
        for n in range(1, zs):
            line_out[q, n - 1] = low[q, lax.rem(z + n, zs)].astype(BF16)
            line_copy(q, n).start()

    def out_copy(q):
        at = pl.ds(q * WIDTH, WIDTH)
        return pltpu.make_async_copy(result.at[q], out_hbm.at[:, at], out_sem.at[q])

    def finish(q):
        at = slice(q * WIDTH, (q + 1) * WIDTH)
        total = low[q, z]
        for n in range(1, zs):
            line_copy(q, n).wait_recv()
            total += line_in[q, n - 1].astype(F32)
        result[q] = base[:, at] - total - earlier[:, at]
        out_copy(q).start()

    top_hops = [[d for d in range(1, zs) if min(d, chunks - 2) == q] for q in range(chunks)]
    own_start(0)
    own_start(1)
    loads[0].wait()
    for p in range(used):
        own_top[p] = panels[used_ref[p]]

    @pl.when((me_s == 0) & (me_i < tops))
    def _():
        for n in range(1, groups):
            hop(n).start()
        top_local().start()

    loads[1].wait()

    def turn(s, carry):
        for n in range(listed):
            turned[s, n * TILE : (n + 1) * TILE, :] = tiles[s, n].T
        return carry

    lax.fori_loop(0, scen_here, turn, 0)
    chain[0] = jnp.zeros(chain.shape[1:], F32)
    loads[2].wait()
    loads[3].wait()

    for q in range(chunks):
        if 1 < q + 1 < chunks:
            own_start(q + 1)
        for d in range(1, zs):
            relay(q, d)
            if q > 0 and d == 1:
                to_groups(q - 1)
            if q > 0 and d == zs - 1:
                to_line(q - 1)
        for d in top_hops[q]:
            pass_on(top_copy, d, has_top)
        if q == 0:

            @pl.when(me_i < tops)
            def _():
                @pl.when(me_s == 0)
                def _():
                    top_local().wait()

                @pl.when(me_s > 0)
                def _():
                    hop(1).wait_recv()

                @pl.when(z < zs - 1)
                def _():
                    top_copy(me_i, 0).start()

                @pl.when(z > 0)
                def _():
                    top_copy(me_i, 1).start()

                top_copy(me_i, 2).start()

        own_local(q).wait()
        for other in range(zs):
            col_copy(q, other * 2 + 1 - c, 2, slot(q, other * 2 + 1 - c)).wait_recv()
        compute(q)
        if q == chunks - 2:
            for other in range(tops // 2):
                top_copy(other * 2 + 1 - c, 2).wait_recv()
            total = jnp.zeros((mine_rows, cols), F32)
            for p in range(used):
                total += lax.dot_general(
                    own_top[p], top[p], (((1,), (1,)), ((), ())), preferred_element_type=F32
                )
            earlier[...] = total
        if q > 1:
            finish(q - 2)
    finish(chunks - 2)
    to_groups(chunks - 1)
    to_line(chunks - 1)
    finish(chunks - 1)

    def drain(copy, other):
        j = other * 2 + c

        @pl.when((z >= other) & (z < zs - 1))
        def _():
            copy(j, 0).wait_send()

        @pl.when((z <= other) & (z > 0))
        def _():
            copy(j, 1).wait_send()

        copy(j, 2).wait_send()

    def drain_chunk(q, carry):
        def one(other, inside):
            drain(lambda j, way: col_copy(q, j, way, slot(q, j)), other)
            return inside

        lax.fori_loop(0, zs, one, 0)
        for n in range(groups):
            pair_copy(q, n).wait_send()
        for n in range(1, groups):
            scen_copy(q, n).wait_send()
        for n in range(1, zs):
            line_copy(q, n).wait_send()
        return carry

    lax.fori_loop(0, chunks, drain_chunk, 0)
    for other in range(tops // 2):
        drain(top_copy, other)

    @pl.when((me_s == 0) & (me_i < tops))
    def _():
        for n in range(1, groups):
            hop(n).wait_send()

    for q in range(chunks):
        out_copy(q).wait()


def on_device(
    groups,
    inner,
    inverse_panels,
    border_columns,
    border_tiles,
    tile_rows,
    tile_slabs,
    tile_count,
    base_slab,
    earlier_panels,
    used_panels,
):
    scen_here, rows, depth = inverse_panels.shape
    cols = border_columns.shape[2]
    listed = border_tiles.shape[1]
    mine_rows = base_slab.shape[0]
    used = used_panels.shape[0]
    nslab = cols // SLAB_W
    chunks = cols // WIDTH
    zs = inner // 2
    sub = TILE // mine_rows
    tops = cols // mine_rows
    entries = scen_here * listed
    targets = mine_rows * groups * inner // TILE * nslab
    live = jnp.arange(listed, dtype=jnp.int32)[None, :] < tile_count[:, None]
    keys = jnp.where(live, tile_rows * nslab + tile_slabs, -1).reshape(entries)
    at = jnp.arange(entries, dtype=jnp.int32)
    same = (keys[None, :] == keys[:, None]) & (at[None, :] < at[:, None])
    prev = jnp.max(jnp.where(same, at[None, :] + 1, 0), axis=1)
    hits = keys[None, :] == jnp.arange(targets, dtype=jnp.int32)[:, None]
    last = jnp.max(jnp.where(hits, at[None, :] + 1, 0), axis=1)
    dma = pltpu.SemaphoreType.DMA
    smem = pl.BlockSpec(memory_space=pltpu.SMEM)
    anywhere = pl.BlockSpec(memory_space=pl.ANY)
    return pl.pallas_call(
        functools.partial(kernel, groups, inner),
        out_shape=jax.ShapeDtypeStruct((mine_rows, cols), F32),
        in_specs=[smem] * 3 + [anywhere] * 5,
        out_specs=anywhere,
        scratch_shapes=[
            pltpu.VMEM((scen_here, rows, depth), BF16),
            pltpu.VMEM((chunks, scen_here, depth, WIDTH), BF16),
            pltpu.VMEM(border_tiles.shape, BF16),
            pltpu.VMEM((scen_here, listed * TILE, rows), BF16),
            pltpu.VMEM((mine_rows, cols), F32),
            pltpu.VMEM(earlier_panels.shape, BF16),
            pltpu.VMEM((used, mine_rows, TILE), BF16),
            pltpu.VMEM((used, cols, TILE), BF16),
            pltpu.VMEM((mine_rows, cols), F32),
            pltpu.VMEM((scen_here, rows, WIDTH), BF16),
            pltpu.VMEM((entries + 1, sub, mine_rows, WIDTH), F32),
            pltpu.VMEM((groups * zs, mine_rows, WIDTH), F32),
            pltpu.VMEM((chunks, groups * zs, mine_rows, WIDTH), F32),
            pltpu.VMEM((chunks, groups * zs, mine_rows, WIDTH), F32),
            pltpu.VMEM((chunks, zs, mine_rows, WIDTH), F32),
            pltpu.VMEM((chunks, groups - 1, zs, mine_rows, WIDTH), BF16),
            pltpu.VMEM((chunks, groups - 1, zs, mine_rows, WIDTH), BF16),
            pltpu.VMEM((chunks, zs, mine_rows, WIDTH), F32),
            pltpu.VMEM((chunks, zs - 1, mine_rows, WIDTH), BF16),
            pltpu.VMEM((chunks, zs - 1, mine_rows, WIDTH), BF16),
            pltpu.VMEM((chunks, mine_rows, WIDTH), F32),
            dma((5,)),
            dma((chunks,)),
            dma((chunks, inner, 3)),
            dma((chunks, inner)),
            dma((groups,)),
            dma,
            dma((tops, 3)),
            dma((tops,)),
            dma((chunks, groups)),
            dma((chunks, groups)),
            dma((chunks, groups - 1)),
            dma((chunks, groups - 1)),
            dma((chunks, zs - 1)),
            dma((chunks, zs - 1)),
            dma((chunks,)),
        ],
        compiler_params=pltpu.CompilerParams(
            collective_id=0, has_side_effects=True, vmem_limit_bytes=60 * 1024 * 1024
        ),
        cost_estimate=pl.CostEstimate(
            flops=2 * scen_here * rows * cols * (depth + listed * TILE // nslab),
            bytes_accessed=2 * scen_here * rows * (depth + listed * TILE + cols),
            transcendentals=0,
        ),
    )(
        used_panels,
        prev,
        last,
        inverse_panels,
        border_columns,
        border_tiles,
        base_slab,
        earlier_panels,
    )


def solution(mesh):
    groups, inner = mesh.shape["scen"], mesh.shape["intr"]
    return jax.shard_map(
        functools.partial(on_device, groups, inner),
        mesh=mesh,
        in_specs=(
            P("scen", "intr", None),
            P("scen", "intr", None),
            P("scen", None, "intr", None),
            P("scen", None),
            P("scen", None),
            P("scen"),
            P(("scen", "intr"), None),
            P(None, ("scen", "intr"), None),
            P(),
        ),
        out_specs=P(("scen", "intr"), None),
        check_vma=False,
    )
```
